128 devices in a mesh: row: 8 (over y_hi, z), col: 16 (over y_lo, x, core).
Axes of the slice: x: 4, y: 4 (y_hi: 2, y_lo: 2; y = y_hi * 2 + y_lo), z: 4, core: 2. Of those that a mesh axis runs over, the one named last changes fastest.
Arguments:
- features: bfloat16 [65536, 256], P(('row', 'col')), may hold values from -6 to 6
- weight: bfloat16 [256, 256], replicated, may hold values from -0.375 to 0.375
- bias_term: float32 [256], replicated, may hold values from -3 to 3
- upstream: bfloat16 [65536, 256], P(('row', 'col')), may hold values from -6 to 6
- block_values: bfloat16 [8, 6144, 128, 128], P('row', 'col'), may hold values from -0.07470703 to 0.07470703
- block_rows: int32 [8, 6144], P('row', 'col'), may hold values from 0 to 63
- block_cols: int32 [8, 6144], P('row', 'col'), may hold values from 0 to 31
- live_count: int32 [8, 16], P('row', 'col'), may hold values from 96 to 384, as said below
Outputs:
- activation: bfloat16 [65536, 256], P(('row', 'col'))
- feature_grad: bfloat16 [65536, 256], P(('row', 'col'))
- weight_grad: float32 [256, 256], replicated
- bias_grad: float32 [256], replicated
The draws below stay inside these ranges and needn't reach their ends.
Inputs may be any that keep to these rules, and one draw needn't show every extreme that they name: `live_count`: every device uses at least a quarter of its slots, and some device uses all 384.
All inputs are finite; a program needn't handle non-finite values.
Results may differ from the reference program's by a relative error of at most 0.007.
Values may be sent and summed in bfloat16 or wider, within the bound.
No kernel may reach another device: no remote copies, remote signals or barrier semaphores. Data moves between devices by JAX's collectives and lax.ppermute only.
A program may use at most 192 MiB of HBM per device.

```python
import jax
import jax.numpy as jnp
from jax import lax

F = 256
BLK = 128
NODE_DEV = 512
NNZB_DEV = 384
NODES = 65536
N_ROW = 8
N_COL = 16
DEVICES = 128


def draw_live_count(key, part):
    key = jax.random.fold_in(key, 11)
    first, second, third, fourth = jax.random.split(key, 4)
    lower = NNZB_DEV // 4
    counts = jnp.minimum(jax.random.randint(first, (N_ROW, N_COL), lower, NNZB_DEV + 1), jax.random.randint(second, (N_ROW, N_COL), lower, NNZB_DEV + 1))
    row_pick = jax.random.randint(third, (), 0, N_ROW)
    col_pick = jax.random.randint(fourth, (), 0, N_COL)
    return counts.at[row_pick, col_pick].set(NNZB_DEV).astype(jnp.int32)


def touch_ends(array, key, smallest, top_value):
    longest = array.shape.index(max(array.shape))
    spots = []
    for shift in (0, 1):
        where = [jax.random.randint(jax.random.fold_in(key, axis), (), 0, length) for axis, length in enumerate(array.shape)]
        where[longest] = (where[longest] + shift) % array.shape[longest]
        spots.append(tuple(where))
    return array.at[spots[0]].set(smallest).at[spots[1]].set(top_value)


def levels(stream_key, extent, cuts, smallest, largest):
    level = 1.0
    for axis_at, parts in cuts:
        steps = jax.random.uniform(jax.random.fold_in(jax.random.fold_in(stream_key, 6), axis_at), (parts,), jnp.float32, smallest / len(cuts), largest / len(cuts))
        level = level * jnp.repeat(jnp.exp(steps), extent[axis_at] // parts).reshape((-1,) + (1,) * (len(extent) - 1 - axis_at))
    return level


def normal_values(rng, dims, width, most, cuts=(), kind=jnp.bfloat16):
    loudness = levels(rng, dims, cuts, -0.22, 0.18) if cuts else 1.0
    result = jax.random.normal(rng, dims, jnp.float32) * width * loudness
    return jnp.minimum(jnp.maximum(result, -most), most).astype(kind)


def setup_inputs(seed: int = 0) -> dict:
    key_of = jax.random.split(jax.random.key(seed), 9)
    return {
        "features": normal_values(key_of[0], (NODES, F), 1.0, 6.0, ((0, 128),)),
        "weight": normal_values(key_of[1], (F, F), F ** -0.5, 0.375),
        "bias_term": normal_values(key_of[2], (F,), 0.5, 3.0, (), jnp.float32),
        "upstream": normal_values(key_of[3], (NODES, F), 1.0, 6.0, ((0, 128),)),
        "block_values": normal_values(key_of[4], (N_ROW, N_COL * NNZB_DEV, BLK, BLK), (0.05 / N_COL ** 0.5), 0.07470703, ((0, 8), (1, 16))),
        "block_rows": touch_ends(jax.random.randint(key_of[5], (N_ROW, N_COL * NNZB_DEV), 0, N_COL * NODE_DEV // BLK), jax.random.fold_in(key_of[5], 1), 0, (N_COL * NODE_DEV // BLK) - 1).astype(jnp.int32),
        "block_cols": touch_ends(jax.random.randint(key_of[6], (N_ROW, N_COL * NNZB_DEV), 0, N_ROW * NODE_DEV // BLK), jax.random.fold_in(key_of[6], 1), 0, (N_ROW * NODE_DEV // BLK) - 1).astype(jnp.int32),
        "live_count": draw_live_count(jax.random.fold_in(key_of[8], 71), 0),
    }


def block_layout(block_rows, block_cols, live_count):
    group_blocks = N_COL * NODE_DEV // BLK
    shard_blocks = NODE_DEV // BLK
    row_ids = jnp.arange(N_ROW, dtype=jnp.int32)[:, None]
    col_ids = (jnp.arange(N_COL * NNZB_DEV, dtype=jnp.int32) // NNZB_DEV)[None, :]
    slot_ids = (jnp.arange(N_COL * NNZB_DEV, dtype=jnp.int32) % NNZB_DEV)[None, :]
    global_rows = row_ids * group_blocks + block_rows
    global_cols = (block_cols // shard_blocks * N_COL + col_ids) * shard_blocks + block_cols % shard_blocks
    limits = live_count[row_ids + 0 * col_ids, col_ids + 0 * row_ids]
    live_mask = (slot_ids < limits).astype(jnp.float32)
    return (global_rows.reshape(-1), global_cols.reshape(-1), live_mask.reshape(-1))

def sparse_apply(block_values, sources, targets, live_mask, field, flipped):
    node_blocks = NODES // BLK
    field_blocks = field.reshape(node_blocks, BLK, F).astype(jnp.float32)
    einsum_form = 'kji,kjf->kif' if flipped else 'kij,kjf->kif'
    steps_total = DEVICES
    grouped = (block_values.reshape(steps_total, NNZB_DEV, BLK, BLK), sources.reshape(steps_total, NNZB_DEV), targets.reshape(steps_total, NNZB_DEV), live_mask.reshape(steps_total, NNZB_DEV))

    def group_step(running, group):
        group_vals, group_sources, group_targets, group_live = group
        pieces = jnp.take(field_blocks, group_sources, axis=0)
        product = jnp.einsum(einsum_form, group_vals.astype(jnp.float32), pieces, precision=lax.Precision.HIGHEST)
        product = product * group_live[:, None, None]
        return (running.at[group_targets].add(product), None)
    initial = jnp.zeros((node_blocks, BLK, F), jnp.float32)
    summed, unused = lax.scan(group_step, initial, grouped)
    return summed.reshape(NODES, F)

def reference(features, weight, bias_term, upstream, block_values, block_rows, block_cols, live_count):
    global_rows, global_cols, live_mask = block_layout(block_rows, block_cols, live_count)
    values_flat = block_values.reshape(N_ROW, N_COL, NNZB_DEV, BLK, BLK).reshape(-1, BLK, BLK)
    aggregated = sparse_apply(values_flat, global_cols, global_rows, live_mask, features, False).astype(jnp.bfloat16)
    preact = jnp.dot(aggregated, weight, preferred_element_type=jnp.float32) + bias_term
    sigmoid_val = jax.nn.sigmoid(preact)
    activation = (preact * sigmoid_val).astype(jnp.bfloat16)
    grad_pre = (upstream.astype(jnp.float32) * sigmoid_val * (1.0 + preact * (1.0 - sigmoid_val))).astype(jnp.bfloat16)
    norm_factor = 1.0 / jnp.sqrt(jnp.float32(NODES))
    weight_grad = jnp.dot(aggregated.T, grad_pre, preferred_element_type=jnp.float32) * norm_factor
    bias_grad = lax.optimization_barrier(jnp.sum(grad_pre.astype(jnp.float32), axis=0)) * norm_factor
    grad_mid = jnp.dot(grad_pre, weight.T, preferred_element_type=jnp.float32).astype(jnp.bfloat16)
    feature_grad = sparse_apply(values_flat, global_rows, global_cols, live_mask, grad_mid, True).astype(jnp.bfloat16)
    return (activation, feature_grad, weight_grad, bias_grad)
```

```python
import functools

import jax
import jax.numpy as jnp
from jax import lax
from jax.experimental import pallas as pl
from jax.experimental.pallas import tpu as pltpu
from jax.sharding import PartitionSpec as P

BF16 = jnp.bfloat16
F32 = jnp.float32
I32 = jnp.int32

F = 256
BLK = 128
SLOTS = 384
STEP = 16
PAIRS = STEP // 2
LOAD = 32
GROUP = 64
PANEL = 32
MIB = 2**20

SMEM_SPEC = pl.BlockSpec(memory_space=pltpu.SMEM)
VMEM_SPEC = pl.BlockSpec(memory_space=pltpu.VMEM)
ANY_SPEC = pl.BlockSpec(memory_space=pl.ANY)


def column(row):
    return jnp.broadcast_to(row, (8, row.shape[1])).T[:, :1]


def sort_slots(unit, bounds, valid, target, source, zero_source, list_ref, tgt_ref):
    shift = unit.bit_length() - 1
    per_step = STEP // unit
    step_shift = per_step.bit_length() - 1
    count = bounds[-1]
    slot = lax.broadcasted_iota(I32, (1, SLOTS), 1)
    target = jnp.where(valid, target, 255)
    earlier = lax.broadcasted_iota(I32, (SLOTS, SLOTS), 0) < lax.broadcasted_iota(
        I32, (SLOTS, SLOTS), 1
    )
    targetf = target.astype(F32)
    same = (column(targetf) == targetf) & earlier
    rank = jnp.sum(jnp.where(same, 1.0, 0.0), axis=0, keepdims=True)
    ids = lax.broadcasted_iota(I32, (count, SLOTS), 0)
    tally = jnp.sum(jnp.where(ids == target, 1.0, 0.0), axis=1, keepdims=True)
    units = ((tally.astype(I32) + (unit - 1)) >> shift).astype(F32)
    offset = jnp.sum(jnp.where(ids < target, units, 0.0), axis=0, keepdims=True)
    local = target
    id_col = lax.broadcasted_iota(I32, (count, 1), 0)
    width = tgt_ref.shape[1]
    where_last = lax.broadcasted_iota(I32, (1, width), 1)
    tail = jnp.zeros((1, width), I32)
    for i, (low, high) in enumerate(zip(bounds, bounds[1:])):
        inside = (id_col >= low) & (id_col < high)
        total = jnp.sum(jnp.where(inside, units, 0.0), axis=0, keepdims=True)
        steps = (total.astype(I32) + (per_step - 1)) >> step_shift
        spare = (steps * per_step).astype(F32) - total
        offset = offset + jnp.where(target >= high, spare, 0.0)
        local = jnp.where((target >= low) & (target < high), target - low, local)
        tail = jnp.where(where_last == width - 4 + i, steps, tail)
    place = jnp.where(valid, unit * offset + rank, -1.0)
    place_col = column(place).astype(I32)
    entry_col = column((slot * 256 + source + 1).astype(F32))
    local_col = column(local.astype(F32))
    at = lax.broadcasted_iota(I32, (SLOTS, list_ref.shape[1]), 1)
    entry = jnp.sum(jnp.where(place_col == at, entry_col, 0.0), axis=0, keepdims=True)
    entry = entry.astype(I32)
    list_ref[...] = jnp.where(entry == 0, zero_source, entry - 1)
    at = lax.broadcasted_iota(I32, (SLOTS, width), 1)
    where = jnp.sum(jnp.where(place_col == unit * at, local_col, 0.0), axis=0, keepdims=True)
    tgt_ref[...] = jnp.where(where_last >= width - 4, tail, where.astype(I32))


def prep_kernel(meta, rows_hbm, cols_hbm, vals, *refs):
    list_a, tgt_a, list_b, tgt_b, held, rows, cols, sems, id_sems = refs
    live, y_hi, z, y_lo, x, core = [meta[i] for i in range(6)]
    ids = [
        pltpu.make_async_copy(rows_hbm, rows, id_sems.at[0]),
        pltpu.make_async_copy(cols_hbm, cols, id_sems.at[1]),
    ]
    chunks = [
        pltpu.make_async_copy(
            vals.at[pl.ds(LOAD * i, LOAD)], held.at[pl.ds(LOAD * i, LOAD)], sems.at[i]
        )
        for i in range(SLOTS // LOAD)
    ]
    for copy in ids:
        copy.start()
    for i, chunk in enumerate(chunks):
        pl.when(LOAD * i < live)(chunk.start)
    for copy in ids:
        copy.wait()

    row = rows[...]
    col = cols[...]
    used = lax.broadcasted_iota(I32, (1, SLOTS), 1) < live
    c = row >> 2
    dcore = (c & 1) ^ core
    dyl = (c >> 3) ^ y_lo
    dx = ((c >> 1) - x) & 3
    q = col >> 2
    dyh = (q >> 2) ^ y_hi
    dz = (q - z) & 3
    near = dyl * 3 + jnp.where(dx == 3, 2, dx)
    own = jnp.where(dx == 2, 32 + dyl * 4, 40 + near * 4)
    row_target = jnp.where(dcore == 1, dyl * 16 + dx * 4, own) + (row & 3)
    order = jnp.where(dz == 2, 0, jnp.where(dz == 0, 1, jnp.where(dz == 1, 2, 3)))
    col_target = jnp.where(dyh == 1, dz * 4, 16 + order * 4) + (col & 3)
    row_early = ((dyl == 0) & (dx != 2)) | ((dyl == 1) & (dx == 0))
    place = jnp.where(row_early, jnp.where(dyl == 1, 3, (dx + 1) >> 1), jnp.where(dyl == 1, dx, 0))
    row_source = dcore * 16 + place * 4 + (row & 3)
    col_early = (dyh == 0) & (dz != 2)
    place = jnp.where(col_early, (dz + 1) >> 1, jnp.where(dyh == 1, 1 + dz, 0))
    col_source = place * 4 + (col & 3)
    row_target = jnp.where(col_early, row_target, 64 + row_target)
    col_target = jnp.where(row_early, col_target, 32 + col_target)
    sort_slots(2, (0, 64, 96, 104, 128), used, row_target, col_source, 20, list_a, tgt_a)
    sort_slots(2, (0, 32, 48, 56, 64), used, col_target, row_source, 32, list_b, tgt_b)

    for i, chunk in enumerate(chunks):
        pl.when(LOAD * i < live)(chunk.wait)


def prep(meta, rows, cols, vals):
    tgts = pltpu.VMEM((1, 384), I32)
    return pl.pallas_call(
        prep_kernel,
        out_shape=(
            pltpu.VMEM((1, 640), I32),
            tgts,
            pltpu.VMEM((1, 640), I32),
            tgts,
            pltpu.VMEM((SLOTS, BLK, BLK), BF16),
        ),
        in_specs=[SMEM_SPEC] + [ANY_SPEC] * 3,
        out_specs=[VMEM_SPEC] * 5,
        scratch_shapes=[
            pltpu.VMEM((1, SLOTS), I32),
            pltpu.VMEM((1, SLOTS), I32),
            pltpu.SemaphoreType.DMA((SLOTS // LOAD,)),
            pltpu.SemaphoreType.DMA((2,)),
        ],
        compiler_params=pltpu.CompilerParams(vmem_limit_bytes=44 * MIB),
        cost_estimate=pl.CostEstimate(
            flops=2**20, bytes_accessed=SLOTS * BLK * BLK * 2, transcendentals=0
        ),
        name="slot_lists",
    )(meta, rows, cols, vals)


def start_pieces(places, pieces, field, sems):
    copies = [
        pltpu.make_async_copy(
            pieces[n].at[pl.ds(first, size)], field.at[pl.ds(to, size)], sems.at[i]
        )
        for i, (n, first, size, to) in enumerate(places)
    ]
    for copy in copies:
        copy.start()
    return copies


PANEL_EARLY = [(0, 0, 4, 0), (1, 0, 4, 4), (2, 0, 4, 8)]
PANEL_LATE = [
    (0, 0, 2, 0),
    (1, 0, 2, 2),
    (2, 0, 4, 4),
    (3, 0, 4, 8),
    (4, 0, 2, 12),
    (5, 0, 2, 14),
    (6, 0, 4, 16),
]
GROUP_EARLY = [(0, 0, 4, 0), (1, 0, 4, 4), (2, 0, 4, 8), (3, 0, 4, 12), (4, 0, 4, 16), (5, 0, 12, 20)]
GROUP_LATE = [
    (0, 0, 4, 4),
    (0, 4, 2, 0),
    (1, 0, 4, 12),
    (1, 4, 2, 2),
    (2, 0, 2, 8),
    (3, 0, 2, 10),
    (4, 0, 4, 20),
    (4, 4, 2, 16),
    (4, 6, 4, 28),
    (4, 10, 2, 18),
    (5, 0, 4, 24),
]


def block_loop(part, forward, list_ref, tgt_ref, held, field, acc):
    tail = tgt_ref.shape[1] - 4
    first = 0
    for i in range(part):
        first = first + tgt_ref[0, tail + i]

    def body(step, _):
        for p in range(PAIRS):
            entries = [list_ref[0, step * STEP + p * 2 + u] for u in range(2)]
            t = tgt_ref[0, step * PAIRS + p]
            blocks = [held[e >> 8] for e in entries]
            fields = [field[e & 255] for e in entries]
            lhs, rhs = (blocks, fields) if forward else (fields, blocks)
            acc[t] += jnp.dot(
                jnp.concatenate(lhs, axis=1),
                jnp.concatenate(rhs, axis=0),
                preferred_element_type=F32,
            )
        return 0

    lax.fori_loop(first, first + tgt_ref[0, tail + part], body, 0)


def clear(acc):
    def step(t, _):
        acc[t] = jnp.zeros(acc.shape[1:], F32)
        return 0

    lax.fori_loop(0, acc.shape[0], step, 0)


def take_over(acc, early, first):
    def step(t, _):
        acc[t] = early[first + t]
        return 0

    lax.fori_loop(0, acc.shape[0], step, 0)


def early_kernel(places, forward, list_ref, tgt_ref, held, *refs):
    *pieces, sums, field, sems = refs
    copies = start_pieces(places, pieces, field, sems)
    last = field.shape[0] - 1
    field[last] = jnp.zeros(field.shape[1:], BF16)
    clear(sums)
    for copy in copies:
        copy.wait()
    block_loop(0, forward, list_ref, tgt_ref, held, field, sums)


def early_product(places, forward, name, sums, field, lists, tgts, held, pieces):
    return pl.pallas_call(
        functools.partial(early_kernel, places, forward),
        out_shape=pltpu.VMEM(sums, F32),
        in_specs=[SMEM_SPEC] * 2 + [VMEM_SPEC] + [ANY_SPEC] * len(pieces),
        out_specs=VMEM_SPEC,
        scratch_shapes=[pltpu.VMEM(field, BF16), pltpu.SemaphoreType.DMA((20,))],
        compiler_params=pltpu.CompilerParams(vmem_limit_bytes=8 * MIB),
        cost_estimate=pl.CostEstimate(
            flops=SLOTS * BLK * BLK * F, bytes_accessed=12 * MIB, transcendentals=0
        ),
        name=name,
    )(lists, tgts, held, *pieces)


def gather_field(places, pieces, field, acc, early, sems):
    copies = start_pieces(places, pieces, field, sems)
    last = field.shape[0] - 1
    field[last] = jnp.zeros(field.shape[1:], BF16)
    take_over(acc, early, 0)
    for copy in copies:
        copy.wait()


def product_call(kernel, name, out_shape, acc_shape, pieces, args):
    count = len(pieces)
    scratch = [pltpu.VMEM(acc_shape, F32)] if acc_shape else []
    if count:
        scratch.append(pltpu.SemaphoreType.DMA((20,)))
    lists, tgts, held, *fields = args
    return pl.pallas_call(
        kernel,
        out_shape=out_shape,
        in_specs=[SMEM_SPEC] * 2
        + [VMEM_SPEC] * (1 + len(fields))
        + [ANY_SPEC] * count,
        out_specs=[VMEM_SPEC] * len(out_shape),
        scratch_shapes=scratch,
        compiler_params=pltpu.CompilerParams(vmem_limit_bytes=10 * MIB),
        cost_estimate=pl.CostEstimate(
            flops=SLOTS * BLK * BLK * F, bytes_accessed=12 * MIB, transcendentals=0
        ),
        name=name,
    )(lists, tgts, held, *fields, *pieces)


def forward_other_kernel(list_ref, tgt_ref, held, early, *refs):
    *pieces, far, near, field, acc, sems = refs
    gather_field(PANEL_LATE, pieces, field, acc, early, sems)
    block_loop(1, True, list_ref, tgt_ref, held, field, acc)

    def store(i, _):
        for dy in range(2):
            far[dy, i] = acc[16 * dy + 8 + i].astype(BF16)
            for n, dx in enumerate((0, 1, 3)):
                near[dy, n, i] = acc[16 * dy + 4 * dx + i].astype(BF16)
        return 0

    lax.fori_loop(0, 4, store, 0)


def forward_other(lists, tgts, held, early, pieces):
    return product_call(
        forward_other_kernel,
        "forward_other_core",
        (
            jax.ShapeDtypeStruct((2, 4, BLK, F), BF16),
            jax.ShapeDtypeStruct((2, 3, 4, BLK, F), BF16),
            pltpu.VMEM((21, BLK, F), BF16),
        ),
        (32, BLK, F),
        pieces,
        (lists, tgts, held, early),
    )


def forward_own_kernel(part, list_ref, tgt_ref, held, early, field, sums):
    take_over(sums, early, (32, 40)[part])
    block_loop(part + 2, True, list_ref, tgt_ref, held, field, sums)


def forward_own(part, lists, tgts, held, early, field):
    return product_call(
        functools.partial(forward_own_kernel, part),
        ("forward_own_far", "forward_own_near")[part],
        (jax.ShapeDtypeStruct(((8, 24)[part], BLK, F), F32),),
        None,
        (),
        (lists, tgts, held, early, field),
    )[0]


WHOLE = jax.ShapeDtypeStruct((4, F, BLK), BF16)
WHOLE_SUM = jax.ShapeDtypeStruct((4, F, BLK), F32)
HALF = jax.ShapeDtypeStruct((2, F, BLK), BF16)


def backward_across_kernel(list_ref, tgt_ref, held, early, *refs):
    *pieces, own, up, down, low, high, field, acc, sems = refs
    gather_field(GROUP_LATE, pieces, field, acc, early, sems)
    block_loop(1, False, list_ref, tgt_ref, held, field, acc)

    def store(i, _):
        own[i] = acc[i]
        up[i] = acc[4 + i].astype(BF16)
        down[i] = acc[12 + i].astype(BF16)
        return 0

    lax.fori_loop(0, 4, store, 0)
    for i in range(2):
        low[i] = acc[8 + i].astype(BF16)
        high[i] = acc[10 + i].astype(BF16)


def backward_across(lists, tgts, held, early, pieces):
    return product_call(
        backward_across_kernel,
        "backward_across",
        (WHOLE_SUM, WHOLE, WHOLE, HALF, HALF, pltpu.VMEM((33, F, BLK), BF16)),
        (16, F, BLK),
        pieces,
        (lists, tgts, held, early),
    )


def backward_far_kernel(list_ref, tgt_ref, held, early, field, low, high, own, acc):
    take_over(acc, early, 16)
    block_loop(2, False, list_ref, tgt_ref, held, field, acc)
    for i in range(2):
        low[i] = acc[i].astype(BF16)
        high[i] = acc[2 + i].astype(BF16)
    for i in range(4):
        own[i] = acc[4 + i]


def backward_far(lists, tgts, held, early, field):
    return product_call(
        backward_far_kernel,
        "backward_far_own",
        (HALF, HALF, WHOLE_SUM),
        (8, F, BLK),
        (),
        (lists, tgts, held, early, field),
    )


def backward_near_kernel(list_ref, tgt_ref, held, early, field, up, down, acc):
    take_over(acc, early, 24)
    block_loop(3, False, list_ref, tgt_ref, held, field, acc)
    for i in range(4):
        up[i] = acc[i].astype(BF16)
        down[i] = acc[4 + i].astype(BF16)


def backward_near(lists, tgts, held, early, field):
    return product_call(
        backward_near_kernel,
        "backward_near",
        (WHOLE, WHOLE),
        (8, F, BLK),
        (),
        (lists, tgts, held, early, field),
    )


def dense_kernel(norm, *refs):
    parts = refs[:4]
    weight, bias, upstream, activation, mid, terms = refs[4:]
    w = weight[...]
    w_term = jnp.zeros((F, F), F32)
    b_term = jnp.zeros((1, F), F32)
    for i in range(4):
        rows = pl.ds(BLK * i, BLK)
        total = parts[0][0, i]
        for part in parts[1:]:
            total = total + part[i].astype(F32)
        aggregated = total.astype(BF16)
        preact = jnp.dot(aggregated, w, preferred_element_type=F32) + bias[...]
        sig = jax.nn.sigmoid(preact)
        activation[rows, :] = (preact * sig).astype(BF16)
        grad_pre = (
            upstream[rows, :].astype(F32) * sig * (1.0 + preact * (1.0 - sig))
        ).astype(BF16)
        mid[i] = lax.dot_general(
            w, grad_pre, (((1,), (1,)), ((), ())), preferred_element_type=F32
        ).astype(BF16)
        w_term += lax.dot_general(
            aggregated, grad_pre, (((0,), (0,)), ((), ())), preferred_element_type=F32
        )
        b_term += jnp.sum(grad_pre.astype(F32), axis=0, keepdims=True)
    terms[pl.ds(0, F), :] = w_term * norm
    terms[pl.ds(F, 8), :] = jnp.broadcast_to(b_term * norm, (8, F))


def dense(parts, weight, bias, upstream, norm):
    return pl.pallas_call(
        functools.partial(dense_kernel, norm),
        out_shape=(
            jax.ShapeDtypeStruct((4 * BLK, F), BF16),
            jax.ShapeDtypeStruct((4, F, BLK), BF16),
            jax.ShapeDtypeStruct((F + 8, F), F32),
        ),
        in_specs=[VMEM_SPEC] * 7,
        out_specs=[VMEM_SPEC] * 3,
        compiler_params=pltpu.CompilerParams(vmem_limit_bytes=12 * MIB),
        cost_estimate=pl.CostEstimate(
            flops=6 * 512 * F * F, bytes_accessed=4 * 2**20, transcendentals=512 * F
        ),
        name="dense_layer",
    )(*parts, weight, bias.reshape(1, F), upstream)


def across_kernel(own, across, out):
    for i in range(4):
        out[i] = own[i] + across[i].astype(F32)


def add_across(own, across):
    return pl.pallas_call(
        across_kernel,
        out_shape=jax.ShapeDtypeStruct(own.shape, F32),
        in_specs=[VMEM_SPEC] * 2,
        out_specs=VMEM_SPEC,
        compiler_params=pltpu.CompilerParams(vmem_limit_bytes=8 * MIB),
        cost_estimate=pl.CostEstimate(flops=10**10, bytes_accessed=MIB, transcendentals=0),
        name="add_across",
    )(own, across)


def finish_kernel(here, up, down, mine, theirs, grad, w_grad, b_grad):
    for i in range(4):
        total = here[i] + (up[i].astype(F32) + down[i].astype(F32))
        grad[pl.ds(BLK * i, BLK), :] = total.T.astype(BF16)
    total = mine[...].astype(F32) + theirs[...].astype(F32)
    w_grad[...] = total[:F]
    b_grad[...] = total[F : F + 1]


def finish(here, up, down, mine, theirs):
    return pl.pallas_call(
        finish_kernel,
        out_shape=(
            jax.ShapeDtypeStruct((4 * BLK, F), BF16),
            jax.ShapeDtypeStruct((F, F), F32),
            jax.ShapeDtypeStruct((1, F), F32),
        ),
        in_specs=[VMEM_SPEC] * 5,
        out_specs=[VMEM_SPEC] * 3,
        compiler_params=pltpu.CompilerParams(vmem_limit_bytes=8 * MIB),
        name="finish_grads",
    )(here, up, down, mine, theirs)


def halves_kernel(*refs):
    up, down, low, high = refs[:4]
    up_out, down_out = refs[-2:]
    for i in range(2):
        up_out[i] = (up[i].astype(F32) + low[i].astype(F32)).astype(BF16)
        up_out[2 + i] = up[2 + i]
        down_out[i] = down[i]
        down_out[2 + i] = (down[2 + i].astype(F32) + high[i].astype(F32)).astype(BF16)
        for extra, out in zip(refs[4:-2], refs[-2:]):
            out[4 + i] = extra[i]


def add_halves(up, down, low, high, *extras):
    blocks = 6 if extras else 4
    return pl.pallas_call(
        halves_kernel,
        out_shape=[jax.ShapeDtypeStruct((blocks, *up.shape[1:]), BF16)] * 2,
        in_specs=[VMEM_SPEC] * (4 + len(extras)),
        out_specs=[VMEM_SPEC] * 2,
        compiler_params=pltpu.CompilerParams(vmem_limit_bytes=8 * MIB),
        cost_estimate=pl.CostEstimate(flops=2**18, bytes_accessed=MIB, transcendentals=0),
        name="add_halves",
    )(up, down, low, high, *extras)


def relay_kernel(keep, got, low, high, up1, down1, up0, down0, own):
    for dy, up, down in ((1, up1, down1), (0, up0, down0)):
        for i in range(4):
            at = 12 * dy + i
            own[dy, i] = keep[at] + got[dy, 0, i].astype(F32)
            right = keep[at + 4] + got[dy, 1, i].astype(F32)
            left = keep[at + 8] + got[dy, 2, i].astype(F32)
            if i < 2:
                right = right + low[dy, i].astype(F32)
            else:
                left = left + high[dy, i - 2].astype(F32)
            up[i] = right.astype(BF16)
            down[i] = left.astype(BF16)


def relay(keep, got, low, high):
    return pl.pallas_call(
        relay_kernel,
        out_shape=[jax.ShapeDtypeStruct((4, BLK, F), BF16)] * 4
        + [jax.ShapeDtypeStruct((2, 4, BLK, F), F32)],
        in_specs=[VMEM_SPEC] * 4,
        out_specs=[VMEM_SPEC] * 5,
        compiler_params=pltpu.CompilerParams(vmem_limit_bytes=8 * MIB),
        cost_estimate=pl.CostEstimate(flops=2**21, bytes_accessed=6 * MIB, transcendentals=0),
        name="relay_sums",
    )(keep, got, low, high)


def from_row(value, dy, dz):
    perm = [((((q >> 2) ^ dy) * 4 + ((q + dz) & 3)), q) for q in range(8)]
    return lax.ppermute(value, "row", perm)


def col_peer(c, dcore, dy, dx):
    return ((c >> 3) ^ dy) * 8 + ((((c >> 1) & 3) + dx) & 3) * 2 + ((c & 1) ^ dcore)


def from_col(value, dcore, dy, dx):
    return lax.ppermute(value, "col", [(col_peer(c, dcore, dy, dx), c) for c in range(16)])


def tie(*values):
    return lax.optimization_barrier(values)


def join(*pieces):
    return jnp.concatenate(pieces, axis=0)


def per_device(
    features, weight, bias_term, upstream, block_values, block_rows, block_cols, live_count
):
    vals = block_values.reshape(SLOTS, BLK, BLK)
    row = lax.axis_index("row")
    col = lax.axis_index("col")
    meta = jnp.stack(
        [live_count[0, 0], row >> 2, row & 3, col >> 3, (col >> 1) & 3, col & 1, row, col]
    ).astype(I32)
    list_a, tgt_a, list_b, tgt_b, held = prep(meta, block_rows, block_cols, vals)

    shard = features.reshape(4, BLK, F)
    other = from_row(shard, 1, 0)
    up, down = from_row(shard, 0, 1), from_row(shard, 0, 3)
    up, down, other, list_a = tie(up, down, other, list_a)
    up2, down2 = from_row(other, 0, 1), from_row(other, 0, 3)
    late = [from_row(up[:2], 0, 1), from_row(down[2:], 0, 3), other]
    early = early_product(
        PANEL_EARLY,
        True,
        "forward_early",
        (64, BLK, F),
        (21, BLK, F),
        list_a,
        tgt_a,
        held,
        (shard, up, down),
    )
    up2, down2, early = tie(up2, down2, early)
    late += [up2, from_row(up2[:2], 0, 1), from_row(down2[2:], 0, 3), down2]

    send_far, send_near, field = forward_other(list_a, tgt_a, held, early, late)
    got_far = from_col(send_far, 1, 0, 0)
    got_near = from_col(send_near, 1, 0, 0)
    keep_far = forward_own(0, list_a, tgt_a, held, early, field)
    far = (keep_far.reshape(2, 4, BLK, F) + got_far.astype(F32)).astype(BF16)
    low, high = far[:, :2], far[:, 2:]
    list_a2, low, high = tie(list_a, low, high)
    low, high = from_col(low, 0, 0, 3), from_col(high, 0, 0, 1)
    keep_near = forward_own(1, list_a2, tgt_a, held, early, field)
    up1, down1, up0, down0, own = relay(keep_near, got_near, low, high)
    up1, down1 = from_col(up1, 0, 0, 3), from_col(down1, 0, 0, 1)
    across = (own[1] + up1.astype(F32) + down1.astype(F32)).astype(BF16)
    up0, down0, across = tie(up0, down0, across)
    across = from_col(across, 0, 1, 0)
    up0, down0 = from_col(up0, 0, 0, 3), from_col(down0, 0, 0, 1)

    nodes = 4 * BLK * lax.axis_size("row") * lax.axis_size("col")
    activation, mid, terms = dense(
        [own, up0, down0, across], weight, bias_term, upstream, float(nodes) ** -0.5
    )

    def pair(value, axis, kind, bit):
        value = value.astype(kind)
        peers = [(i ^ bit, i) for i in range(lax.axis_size(axis))]
        return value, lax.ppermute(value, axis, peers)

    def add(mine, theirs):
        return mine.astype(F32) + theirs.astype(F32)

    def core(value):
        return from_col(value, 1, 0, 0)

    up, down = from_col(mid, 0, 0, 1), from_col(mid, 0, 0, 3)
    other = from_col(mid, 0, 1, 0)
    terms1 = add(*pair(terms, "col", F32, 1))
    other, terms1 = tie(other, terms1)
    mine, theirs = pair(terms1, "row", F32, 1)
    up2 = from_col(join(other, up[:2]), 0, 0, 1)
    down2 = from_col(join(other, down[2:]), 0, 0, 3)
    mates = [core(mid), core(join(up, down, other))]
    early = early_product(
        GROUP_EARLY,
        False,
        "backward_early",
        (32, F, BLK),
        (33, F, BLK),
        list_b,
        tgt_b,
        held,
        (mid, up, down, other, *mates),
    )
    up2, down2, theirs, early = tie(up2, down2, theirs, early)
    up2, down2, terms2 = tie(up2, down2, add(mine, theirs))
    mine, theirs = pair(terms2, "col", F32, 8)
    low, high = from_col(up2[:2], 0, 0, 1), from_col(down2[2:4], 0, 0, 3)
    late = [up2, down2, low, high, core(join(up2, down2)), core(join(low, high))]
    list_b1, terms3 = tie(list_b, add(mine, theirs))
    mine, theirs = pair(terms3, "row", BF16, 2)

    own1, up1, down1, low1, high1, field = backward_across(list_b1, tgt_b, held, early, late)
    theirs, own1 = tie(theirs, own1)
    terms4 = add(mine, theirs)
    low1, high1 = from_row(low1, 0, 3), from_row(high1, 0, 1)
    mine, theirs = pair(terms4, "row", BF16, 4)
    low0, high0, own0 = backward_far(list_b, tgt_b, held, early, field)
    up1, down1, own0 = tie(up1, down1, own0)
    up1, down1 = add_halves(up1, down1, low1, high1, low0, high0)
    theirs, up1, down1 = tie(theirs, up1, down1)
    list_b2, terms5 = tie(list_b, add(mine, theirs))
    up1, down1 = from_row(up1, 0, 3), from_row(down1, 0, 1)
    mine, theirs = pair(terms5, "col", BF16, 2)
    up0, down0 = backward_near(list_b2, tgt_b, held, early, field)
    up1, down1, up0, theirs = tie(up1, down1, up0, theirs)
    across = (own1 + up1[:4].astype(F32) + down1[:4].astype(F32)).astype(BF16)
    across = from_row(across, 1, 0)
    up0, down0 = add_halves(up0, down0, up1[4:], down1[4:])
    up0, down0 = from_row(up0, 0, 3), from_row(down0, 0, 1)
    mine, theirs = pair(add(mine, theirs), "col", BF16, 4)
    here = add_across(own0, across)
    feature_grad, weight_grad, bias_grad = finish(here, up0, down0, mine, theirs)
    return (activation, feature_grad, weight_grad, bias_grad.reshape(F))


def solution(mesh):
    in_specs = (
        P(("row", "col"), None),
        P(),
        P(),
        P(("row", "col"), None),
        P("row", "col", None, None),
        P("row", "col"),
        P("row", "col"),
        P("row", "col"),
    )
    out_specs = (P(("row", "col"), None), P(("row", "col"), None), P(), P())
    return jax.shard_map(
        per_device, mesh=mesh, in_specs=in_specs, out_specs=out_specs, check_vma=False
    )
```

```python
import functools

import jax
import jax.numpy as jnp
from jax import lax
from jax.experimental import pallas as pl
from jax.experimental.pallas import tpu as pltpu
from jax.sharding import PartitionSpec as P

BF16 = jnp.bfloat16
F32 = jnp.float32
I32 = jnp.int32

F = 256
BLK = 128
SLOTS = 384
STEP = 16
PAIRS = STEP // 2
LOAD = 32
GROUP = 64
PANEL = 32
MIB = 2**20

SMEM_SPEC = pl.BlockSpec(memory_space=pltpu.SMEM)
VMEM_SPEC = pl.BlockSpec(memory_space=pltpu.VMEM)
ANY_SPEC = pl.BlockSpec(memory_space=pl.ANY)


def column(row):
    return jnp.broadcast_to(row, (8, row.shape[1])).T[:, :1]


def sort_slots(unit, bounds, valid, target, source, zero_source, list_ref, tgt_ref):
    shift = unit.bit_length() - 1
    per_step = STEP // unit
    step_shift = per_step.bit_length() - 1
    count = bounds[-1]
    slot = lax.broadcasted_iota(I32, (1, SLOTS), 1)
    target = jnp.where(valid, target, 255)
    earlier = lax.broadcasted_iota(I32, (SLOTS, SLOTS), 0) < lax.broadcasted_iota(
        I32, (SLOTS, SLOTS), 1
    )
    targetf = target.astype(F32)
    same = (column(targetf) == targetf) & earlier
    rank = jnp.sum(jnp.where(same, 1.0, 0.0), axis=0, keepdims=True)
    ids = lax.broadcasted_iota(I32, (count, SLOTS), 0)
    tally = jnp.sum(jnp.where(ids == target, 1.0, 0.0), axis=1, keepdims=True)
    units = ((tally.astype(I32) + (unit - 1)) >> shift).astype(F32)
    offset = jnp.sum(jnp.where(ids < target, units, 0.0), axis=0, keepdims=True)
    local = target
    id_col = lax.broadcasted_iota(I32, (count, 1), 0)
    width = tgt_ref.shape[1]
    where_last = lax.broadcasted_iota(I32, (1, width), 1)
    tail = jnp.zeros((1, width), I32)
    for i, (low, high) in enumerate(zip(bounds, bounds[1:])):
        inside = (id_col >= low) & (id_col < high)
        total = jnp.sum(jnp.where(inside, units, 0.0), axis=0, keepdims=True)
        steps = (total.astype(I32) + (per_step - 1)) >> step_shift
        spare = (steps * per_step).astype(F32) - total
        offset = offset + jnp.where(target >= high, spare, 0.0)
        local = jnp.where((target >= low) & (target < high), target - low, local)
        tail = jnp.where(where_last == width - 4 + i, steps, tail)
    place = jnp.where(valid, unit * offset + rank, -1.0)
    place_col = column(place).astype(I32)
    entry_col = column((slot * 256 + source + 1).astype(F32))
    local_col = column(local.astype(F32))
    at = lax.broadcasted_iota(I32, (SLOTS, list_ref.shape[1]), 1)
    entry = jnp.sum(jnp.where(place_col == at, entry_col, 0.0), axis=0, keepdims=True)
    entry = entry.astype(I32)
    list_ref[...] = jnp.where(entry == 0, zero_source, entry - 1)
    at = lax.broadcasted_iota(I32, (SLOTS, width), 1)
    where = jnp.sum(jnp.where(place_col == unit * at, local_col, 0.0), axis=0, keepdims=True)
    tgt_ref[...] = jnp.where(where_last >= width - 4, tail, where.astype(I32))


def list_kernel(forward, meta, rows, cols, *refs):
    live, y_hi, z, y_lo, x, core = [meta[i] for i in range(6)]
    chunks = []
    if forward:
        vals, list_ref, tgt_ref, held, sems = refs
        chunks = [
            pltpu.make_async_copy(
                vals.at[pl.ds(LOAD * i, LOAD)], held.at[pl.ds(LOAD * i, LOAD)], sems.at[i]
            )
            for i in range(SLOTS // LOAD)
        ]
    else:
        list_ref, tgt_ref = refs
    for i, chunk in enumerate(chunks):
        pl.when(LOAD * i < live)(chunk.start)
    row = rows[...]
    col = cols[...]
    used = lax.broadcasted_iota(I32, (1, SLOTS), 1) < live
    c = row >> 2
    dcore = (c & 1) ^ core
    dyl = (c >> 3) ^ y_lo
    dx = ((c >> 1) - x) & 3
    q = col >> 2
    dyh = (q >> 2) ^ y_hi
    dz = (q - z) & 3
    near = dyl * 3 + jnp.where(dx == 3, 2, dx)
    own = jnp.where(dx == 2, 32 + dyl * 4, 40 + near * 4)
    row_target = jnp.where(dcore == 1, dyl * 16 + dx * 4, own) + (row & 3)
    order = jnp.where(dz == 2, 0, jnp.where(dz == 0, 1, jnp.where(dz == 1, 2, 3)))
    col_target = jnp.where(dyh == 1, dz * 4, 16 + order * 4) + (col & 3)
    row_early = ((dyl == 0) & (dx != 2)) | ((dyl == 1) & (dx == 0))
    place = jnp.where(row_early, jnp.where(dyl == 1, 3, (dx + 1) >> 1), jnp.where(dyl == 1, dx, 0))
    row_source = dcore * 16 + place * 4 + (row & 3)
    col_early = (dyh == 0) & (dz != 2)
    place = jnp.where(col_early, (dz + 1) >> 1, jnp.where(dyh == 1, 1 + dz, 0))
    col_source = place * 4 + (col & 3)
    if forward:
        target = jnp.where(col_early, row_target, 64 + row_target)
        sort_slots(2, (0, 64, 96, 104, 128), used, target, col_source, 20, list_ref, tgt_ref)
    else:
        target = jnp.where(row_early, col_target, 32 + col_target)
        sort_slots(2, (0, 32, 48, 56, 64), used, target, row_source, 32, list_ref, tgt_ref)
    for i, chunk in enumerate(chunks):
        pl.when(LOAD * i < live)(chunk.wait)


def slot_list(meta, rows, cols, vals=None):
    forward = vals is not None
    out = [pltpu.VMEM((1, 640), I32), pltpu.VMEM((1, 384), I32)]
    if forward:
        out.append(pltpu.VMEM((SLOTS, BLK, BLK), BF16))
    return pl.pallas_call(
        functools.partial(list_kernel, forward),
        out_shape=out,
        in_specs=[SMEM_SPEC, VMEM_SPEC, VMEM_SPEC] + [ANY_SPEC] * forward,
        out_specs=[VMEM_SPEC] * len(out),
        scratch_shapes=[pltpu.SemaphoreType.DMA((SLOTS // LOAD,))] * forward,
        compiler_params=pltpu.CompilerParams(vmem_limit_bytes=(44 if forward else 8) * MIB),
        cost_estimate=pl.CostEstimate(flops=2**20, bytes_accessed=8 * MIB, transcendentals=0),
        name="slot_list_forward" if forward else "slot_list_backward",
    )(meta, rows, cols, *([vals] if forward else []))


def start_pieces(places, pieces, field, sems):
    copies = [
        pltpu.make_async_copy(
            pieces[n].at[pl.ds(first, size)], field.at[pl.ds(to, size)], sems.at[i]
        )
        for i, (n, first, size, to) in enumerate(places)
    ]
    for copy in copies:
        copy.start()
    return copies


PANEL_EARLY = [(0, 0, 4, 0), (1, 0, 4, 4), (2, 0, 4, 8)]
PANEL_LATE = [
    (0, 0, 2, 0),
    (1, 0, 2, 2),
    (2, 0, 4, 4),
    (3, 0, 4, 8),
    (4, 0, 2, 12),
    (5, 0, 2, 14),
    (6, 0, 4, 16),
]
GROUP_EARLY = [(0, 0, 4, 0), (1, 0, 4, 4), (2, 0, 4, 8), (3, 0, 4, 12), (4, 0, 4, 16), (5, 0, 12, 20)]
GROUP_LATE = [
    (0, 0, 4, 4),
    (0, 4, 2, 0),
    (1, 0, 4, 12),
    (1, 4, 2, 2),
    (2, 0, 2, 8),
    (3, 0, 2, 10),
    (4, 0, 4, 20),
    (4, 4, 2, 16),
    (4, 6, 4, 28),
    (4, 10, 2, 18),
    (5, 0, 4, 24),
]


def block_loop(part, forward, list_ref, tgt_ref, held, field, acc):
    tail = tgt_ref.shape[1] - 4
    first = 0
    for i in range(part):
        first = first + tgt_ref[0, tail + i]

    def body(step, _):
        for p in range(PAIRS):
            entries = [list_ref[0, step * STEP + p * 2 + u] for u in range(2)]
            t = tgt_ref[0, step * PAIRS + p]
            blocks = [held[e >> 8] for e in entries]
            fields = [field[e & 255] for e in entries]
            lhs, rhs = (blocks, fields) if forward else (fields, blocks)
            acc[t] += jnp.dot(
                jnp.concatenate(lhs, axis=1),
                jnp.concatenate(rhs, axis=0),
                preferred_element_type=F32,
            )
        return 0

    lax.fori_loop(first, first + tgt_ref[0, tail + part], body, 0)


def clear(acc):
    def step(t, _):
        acc[t] = jnp.zeros(acc.shape[1:], F32)
        return 0

    lax.fori_loop(0, acc.shape[0], step, 0)


def take_over(acc, early, first):
    def step(t, _):
        acc[t] = early[first + t]
        return 0

    lax.fori_loop(0, acc.shape[0], step, 0)


def early_kernel(places, forward, list_ref, tgt_ref, held, *refs):
    *pieces, sums, field, sems = refs
    copies = start_pieces(places, pieces, field, sems)
    last = field.shape[0] - 1
    field[last] = jnp.zeros(field.shape[1:], BF16)
    clear(sums)
    for copy in copies:
        copy.wait()
    block_loop(0, forward, list_ref, tgt_ref, held, field, sums)


def early_product(places, forward, name, sums, field, lists, tgts, held, pieces):
    return pl.pallas_call(
        functools.partial(early_kernel, places, forward),
        out_shape=pltpu.VMEM(sums, F32),
        in_specs=[SMEM_SPEC] * 2 + [VMEM_SPEC] + [ANY_SPEC] * len(pieces),
        out_specs=VMEM_SPEC,
        scratch_shapes=[pltpu.VMEM(field, BF16), pltpu.SemaphoreType.DMA((20,))],
        compiler_params=pltpu.CompilerParams(vmem_limit_bytes=8 * MIB),
        cost_estimate=pl.CostEstimate(
            flops=SLOTS * BLK * BLK * F, bytes_accessed=12 * MIB, transcendentals=0
        ),
        name=name,
    )(lists, tgts, held, *pieces)


def gather_field(places, pieces, field, acc, early, sems):
    copies = start_pieces(places, pieces, field, sems)
    last = field.shape[0] - 1
    field[last] = jnp.zeros(field.shape[1:], BF16)
    take_over(acc, early, 0)
    for copy in copies:
        copy.wait()


def product_call(kernel, name, out_shape, acc_shape, pieces, args):
    count = len(pieces)
    scratch = [pltpu.VMEM(acc_shape, F32)] if acc_shape else []
    if count:
        scratch.append(pltpu.SemaphoreType.DMA((20,)))
    lists, tgts, held, *fields = args
    return pl.pallas_call(
        kernel,
        out_shape=out_shape,
        in_specs=[SMEM_SPEC] * 2
        + [VMEM_SPEC] * (1 + len(fields))
        + [ANY_SPEC] * count,
        out_specs=[VMEM_SPEC] * len(out_shape),
        scratch_shapes=scratch,
        compiler_params=pltpu.CompilerParams(vmem_limit_bytes=10 * MIB),
        cost_estimate=pl.CostEstimate(
            flops=SLOTS * BLK * BLK * F, bytes_accessed=12 * MIB, transcendentals=0
        ),
        name=name,
    )(lists, tgts, held, *fields, *pieces)


def forward_other_kernel(list_ref, tgt_ref, held, early, *refs):
    *pieces, far, near, field, acc, sems = refs
    gather_field(PANEL_LATE, pieces, field, acc, early, sems)
    block_loop(1, True, list_ref, tgt_ref, held, field, acc)

    def store(i, _):
        for dy in range(2):
            far[dy, i] = acc[16 * dy + 8 + i].astype(BF16)
            for n, dx in enumerate((0, 1, 3)):
                near[dy, n, i] = acc[16 * dy + 4 * dx + i].astype(BF16)
        return 0

    lax.fori_loop(0, 4, store, 0)


def forward_other(lists, tgts, held, early, pieces):
    return product_call(
        forward_other_kernel,
        "forward_other_core",
        (
            jax.ShapeDtypeStruct((2, 4, BLK, F), BF16),
            jax.ShapeDtypeStruct((2, 3, 4, BLK, F), BF16),
            pltpu.VMEM((21, BLK, F), BF16),
        ),
        (32, BLK, F),
        pieces,
        (lists, tgts, held, early),
    )


def forward_own_kernel(part, list_ref, tgt_ref, held, early, field, sums):
    take_over(sums, early, (32, 40)[part])
    block_loop(part + 2, True, list_ref, tgt_ref, held, field, sums)


def forward_own(part, lists, tgts, held, early, field):
    return product_call(
        functools.partial(forward_own_kernel, part),
        ("forward_own_far", "forward_own_near")[part],
        (jax.ShapeDtypeStruct(((8, 24)[part], BLK, F), F32),),
        None,
        (),
        (lists, tgts, held, early, field),
    )[0]


WHOLE = jax.ShapeDtypeStruct((4, F, BLK), BF16)
WHOLE_SUM = jax.ShapeDtypeStruct((4, F, BLK), F32)
HALF = jax.ShapeDtypeStruct((2, F, BLK), BF16)


def backward_across_kernel(list_ref, tgt_ref, held, early, *refs):
    *pieces, own, up, down, low, high, field, acc, sems = refs
    gather_field(GROUP_LATE, pieces, field, acc, early, sems)
    block_loop(1, False, list_ref, tgt_ref, held, field, acc)

    def store(i, _):
        own[i] = acc[i]
        up[i] = acc[4 + i].astype(BF16)
        down[i] = acc[12 + i].astype(BF16)
        return 0

    lax.fori_loop(0, 4, store, 0)
    for i in range(2):
        low[i] = acc[8 + i].astype(BF16)
        high[i] = acc[10 + i].astype(BF16)


def backward_across(lists, tgts, held, early, pieces):
    return product_call(
        backward_across_kernel,
        "backward_across",
        (WHOLE_SUM, WHOLE, WHOLE, HALF, HALF, pltpu.VMEM((33, F, BLK), BF16)),
        (16, F, BLK),
        pieces,
        (lists, tgts, held, early),
    )


def backward_far_kernel(list_ref, tgt_ref, held, early, field, low, high, own, acc):
    take_over(acc, early, 16)
    block_loop(2, False, list_ref, tgt_ref, held, field, acc)
    for i in range(2):
        low[i] = acc[i].astype(BF16)
        high[i] = acc[2 + i].astype(BF16)
    for i in range(4):
        own[i] = acc[4 + i]


def backward_far(lists, tgts, held, early, field):
    return product_call(
        backward_far_kernel,
        "backward_far_own",
        (HALF, HALF, WHOLE_SUM),
        (8, F, BLK),
        (),
        (lists, tgts, held, early, field),
    )


def backward_near_kernel(list_ref, tgt_ref, held, early, field, up, down, acc):
    take_over(acc, early, 24)
    block_loop(3, False, list_ref, tgt_ref, held, field, acc)
    for i in range(4):
        up[i] = acc[i].astype(BF16)
        down[i] = acc[4 + i].astype(BF16)


def backward_near(lists, tgts, held, early, field):
    return product_call(
        backward_near_kernel,
        "backward_near",
        (WHOLE, WHOLE),
        (8, F, BLK),
        (),
        (lists, tgts, held, early, field),
    )


def dense_kernel(norm, *refs):
    parts = refs[:4]
    meta, weight, bias, upstream, activation, mid, keep, send, scratch = refs[4:]
    w = weight[...]
    w_term = jnp.zeros((F, F), F32)
    b_term = jnp.zeros((1, F), F32)
    for i in range(4):
        rows = pl.ds(BLK * i, BLK)
        total = parts[0][0, i]
        for part in parts[1:]:
            total = total + part[i].astype(F32)
        aggregated = total.astype(BF16)
        preact = jnp.dot(aggregated, w, preferred_element_type=F32) + bias[...]
        sig = jax.nn.sigmoid(preact)
        activation[rows, :] = (preact * sig).astype(BF16)
        grad_pre = (
            upstream[rows, :].astype(F32) * sig * (1.0 + preact * (1.0 - sig))
        ).astype(BF16)
        mid[i] = lax.dot_general(
            w, grad_pre, (((1,), (1,)), ((), ())), preferred_element_type=F32
        ).astype(BF16)
        w_term += lax.dot_general(
            aggregated, grad_pre, (((0,), (0,)), ((), ())), preferred_element_type=F32
        )
        b_term += jnp.sum(grad_pre.astype(F32), axis=0, keepdims=True)
    scratch[...] = w_term * norm
    core = meta[5]
    b_rows = jnp.broadcast_to(b_term * norm, (8, F))
    for half, which in ((keep, core), (send, 1 - core)):
        half[pl.ds(0, BLK), :] = scratch[pl.ds(pl.multiple_of(which * BLK, BLK), BLK), :]
        half[pl.ds(BLK, 8), :] = b_rows


def dense(parts, meta, weight, bias, upstream, norm):
    return pl.pallas_call(
        functools.partial(dense_kernel, norm),
        out_shape=(
            jax.ShapeDtypeStruct((4 * BLK, F), BF16),
            jax.ShapeDtypeStruct((4, F, BLK), BF16),
            jax.ShapeDtypeStruct((BLK + 8, F), F32),
            jax.ShapeDtypeStruct((BLK + 8, F), F32),
        ),
        in_specs=[VMEM_SPEC] * 4 + [SMEM_SPEC] + [VMEM_SPEC] * 3,
        out_specs=[VMEM_SPEC] * 4,
        scratch_shapes=[pltpu.VMEM((F, F), F32)],
        compiler_params=pltpu.CompilerParams(vmem_limit_bytes=12 * MIB),
        cost_estimate=pl.CostEstimate(
            flops=6 * 512 * F * F, bytes_accessed=4 * 2**20, transcendentals=512 * F
        ),
        name="dense_layer",
    )(*parts, meta, weight, bias.reshape(1, F), upstream)


def across_kernel(own, across, out):
    for i in range(4):
        out[i] = own[i] + across[i].astype(F32)


def add_across(own, across):
    return pl.pallas_call(
        across_kernel,
        out_shape=jax.ShapeDtypeStruct(own.shape, F32),
        in_specs=[VMEM_SPEC] * 2,
        out_specs=VMEM_SPEC,
        compiler_params=pltpu.CompilerParams(vmem_limit_bytes=8 * MIB),
        cost_estimate=pl.CostEstimate(flops=4 * 10**10, bytes_accessed=MIB, transcendentals=0),
        name="add_across",
    )(own, across)


def finish_kernel(here, up, down, meta, *refs):
    mine, theirs, mate, mate_theirs, grad, w_grad, b_grad = refs
    for i in range(4):
        total = here[i] + (up[i].astype(F32) + down[i].astype(F32))
        grad[pl.ds(BLK * i, BLK), :] = total.T.astype(BF16)
    core = meta[5]
    for one, two, which in ((mine, theirs, core), (mate, mate_theirs, 1 - core)):
        total = one[...].astype(F32) + two[...].astype(F32)
        w_grad[pl.ds(pl.multiple_of(which * BLK, BLK), BLK), :] = total[:BLK]
    b_grad[...] = total[BLK : BLK + 1]


def finish(here, up, down, meta, *terms):
    return pl.pallas_call(
        finish_kernel,
        out_shape=(
            jax.ShapeDtypeStruct((4 * BLK, F), BF16),
            jax.ShapeDtypeStruct((F, F), F32),
            jax.ShapeDtypeStruct((1, F), F32),
        ),
        in_specs=[VMEM_SPEC] * 3 + [SMEM_SPEC] + [VMEM_SPEC] * 4,
        out_specs=[VMEM_SPEC] * 3,
        compiler_params=pltpu.CompilerParams(vmem_limit_bytes=8 * MIB),
        name="finish_grads",
    )(here, up, down, meta, *terms)


def halves_kernel(*refs):
    up, down, low, high = refs[:4]
    up_out, down_out = refs[-2:]
    for i in range(2):
        up_out[i] = (up[i].astype(F32) + low[i].astype(F32)).astype(BF16)
        up_out[2 + i] = up[2 + i]
        down_out[i] = down[i]
        down_out[2 + i] = (down[2 + i].astype(F32) + high[i].astype(F32)).astype(BF16)
        for extra, out in zip(refs[4:-2], refs[-2:]):
            out[4 + i] = extra[i]


def add_halves(up, down, low, high, *extras):
    blocks = 6 if extras else 4
    return pl.pallas_call(
        halves_kernel,
        out_shape=[jax.ShapeDtypeStruct((blocks, *up.shape[1:]), BF16)] * 2,
        in_specs=[VMEM_SPEC] * (4 + len(extras)),
        out_specs=[VMEM_SPEC] * 2,
        compiler_params=pltpu.CompilerParams(vmem_limit_bytes=8 * MIB),
        cost_estimate=pl.CostEstimate(flops=2**18, bytes_accessed=MIB, transcendentals=0),
        name="add_halves",
    )(up, down, low, high, *extras)


def relay_kernel(keep, got, low, high, up1, down1, up0, down0, own):
    for dy, up, down in ((1, up1, down1), (0, up0, down0)):
        for i in range(4):
            at = 12 * dy + i
            own[dy, i] = keep[at] + got[dy, 0, i].astype(F32)
            right = keep[at + 4] + got[dy, 1, i].astype(F32)
            left = keep[at + 8] + got[dy, 2, i].astype(F32)
            if i < 2:
                right = right + low[dy, i].astype(F32)
            else:
                left = left + high[dy, i - 2].astype(F32)
            up[i] = right.astype(BF16)
            down[i] = left.astype(BF16)


def relay(keep, got, low, high):
    return pl.pallas_call(
        relay_kernel,
        out_shape=[jax.ShapeDtypeStruct((4, BLK, F), BF16)] * 4
        + [jax.ShapeDtypeStruct((2, 4, BLK, F), F32)],
        in_specs=[VMEM_SPEC] * 4,
        out_specs=[VMEM_SPEC] * 5,
        compiler_params=pltpu.CompilerParams(vmem_limit_bytes=8 * MIB),
        cost_estimate=pl.CostEstimate(flops=2**21, bytes_accessed=6 * MIB, transcendentals=0),
        name="relay_sums",
    )(keep, got, low, high)


def from_row(value, dy, dz):
    perm = [((((q >> 2) ^ dy) * 4 + ((q + dz) & 3)), q) for q in range(8)]
    return lax.ppermute(value, "row", perm)


def col_peer(c, dcore, dy, dx):
    return ((c >> 3) ^ dy) * 8 + ((((c >> 1) & 3) + dx) & 3) * 2 + ((c & 1) ^ dcore)


def from_col(value, dcore, dy, dx):
    return lax.ppermute(value, "col", [(col_peer(c, dcore, dy, dx), c) for c in range(16)])


def tie(*values):
    return lax.optimization_barrier(values)


def join(*pieces):
    return jnp.concatenate(pieces, axis=0)


def per_device(
    features, weight, bias_term, upstream, block_values, block_rows, block_cols, live_count
):
    vals = block_values.reshape(SLOTS, BLK, BLK)
    row = lax.axis_index("row")
    col = lax.axis_index("col")
    meta = jnp.stack(
        [live_count[0, 0], row >> 2, row & 3, col >> 3, (col >> 1) & 3, col & 1, row, col]
    ).astype(I32)
    shard = features.reshape(4, BLK, F)
    list_a, tgt_a, held = slot_list(meta, block_rows, block_cols, vals)
    list_b, tgt_b = slot_list(meta, block_rows, block_cols)

    other = from_row(shard, 1, 0)
    up, down = from_row(shard, 0, 1), from_row(shard, 0, 3)
    other, up, down, list_a = tie(other, up, down, list_a)
    up2, down2 = from_row(other, 0, 1), from_row(other, 0, 3)
    late = [from_row(up[:2], 0, 1), from_row(down[2:], 0, 3), other]
    early = early_product(
        PANEL_EARLY,
        True,
        "forward_early",
        (64, BLK, F),
        (21, BLK, F),
        list_a,
        tgt_a,
        held,
        (shard, up, down),
    )
    up2, down2, early = tie(up2, down2, early)
    late += [up2, from_row(up2[:2], 0, 1), from_row(down2[2:], 0, 3), down2]

    send_far, send_near, field = forward_other(list_a, tgt_a, held, early, late)
    got_far = from_col(send_far, 1, 0, 0)
    got_near = from_col(send_near, 1, 0, 0)
    keep_far = forward_own(0, list_a, tgt_a, held, early, field)
    far = (keep_far.reshape(2, 4, BLK, F) + got_far.astype(F32)).astype(BF16)
    low, high = far[:, :2], far[:, 2:]
    list_a2, low, high = tie(list_a, low, high)
    low, high = from_col(low, 0, 0, 3), from_col(high, 0, 0, 1)
    keep_near = forward_own(1, list_a2, tgt_a, held, early, field)
    up1, down1, up0, down0, own = relay(keep_near, got_near, low, high)
    up1, down1 = from_col(up1, 0, 0, 3), from_col(down1, 0, 0, 1)
    across = (own[1] + up1.astype(F32) + down1.astype(F32)).astype(BF16)
    up0, down0, across, list_b = tie(up0, down0, across, list_b)
    across = from_col(across, 0, 1, 0)
    up0, down0 = from_col(up0, 0, 0, 3), from_col(down0, 0, 0, 1)

    nodes = 4 * BLK * lax.axis_size("row") * lax.axis_size("col")
    activation, mid, keep, send = dense(
        [own, up0, down0, across], meta, weight, bias_term, upstream, float(nodes) ** -0.5
    )

    def pair(value, axis, kind, bit):
        value = value.astype(kind)
        peers = [(i ^ bit, i) for i in range(lax.axis_size(axis))]
        return value, lax.ppermute(value, axis, peers)

    def add(mine, theirs):
        return mine.astype(F32) + theirs.astype(F32)

    def core(value):
        return from_col(value, 1, 0, 0)

    up, down = from_col(mid, 0, 0, 1), from_col(mid, 0, 0, 3)
    other = from_col(mid, 0, 1, 0)
    terms1 = keep + core(send)
    other, terms1 = tie(other, terms1)
    mine, theirs = pair(terms1, "row", F32, 1)
    up2 = from_col(join(other, up[:2]), 0, 0, 1)
    down2 = from_col(join(other, down[2:]), 0, 0, 3)
    mates = [core(mid), core(join(up, down, other))]
    early = early_product(
        GROUP_EARLY,
        False,
        "backward_early",
        (32, F, BLK),
        (33, F, BLK),
        list_b,
        tgt_b,
        held,
        (mid, up, down, other, *mates),
    )
    up2, down2, theirs, early = tie(up2, down2, theirs, early)
    up2, down2, terms2 = tie(up2, down2, add(mine, theirs))
    mine, theirs = pair(terms2, "col", F32, 8)
    low, high = from_col(up2[:2], 0, 0, 1), from_col(down2[2:4], 0, 0, 3)
    low, high, theirs = tie(low, high, theirs)
    late = [up2, down2, low, high, core(join(up2, down2)), core(join(low, high))]
    list_b1, terms3 = tie(list_b, add(mine, theirs))
    mine, theirs = pair(terms3, "row", BF16, 2)

    own1, up1, down1, low1, high1, field = backward_across(list_b1, tgt_b, held, early, late)
    theirs, own1 = tie(theirs, own1)
    terms4 = add(mine, theirs)
    low1, high1 = from_row(low1, 0, 3), from_row(high1, 0, 1)
    mine, theirs = pair(terms4, "row", BF16, 4)
    low0, high0, own0 = backward_far(list_b, tgt_b, held, early, field)
    up1, down1, own0 = tie(up1, down1, own0)
    up1, down1 = add_halves(up1, down1, low1, high1, low0, high0)
    theirs, up1, down1 = tie(theirs, up1, down1)
    list_b2, terms5 = tie(list_b, add(mine, theirs))
    up1, down1 = from_row(up1, 0, 3), from_row(down1, 0, 1)
    mine, theirs = pair(terms5, "col", BF16, 2)
    up0, down0 = backward_near(list_b2, tgt_b, held, early, field)
    up1, down1, up0, theirs = tie(up1, down1, up0, theirs)
    across = (own1 + up1[:4].astype(F32) + down1[:4].astype(F32)).astype(BF16)
    across = from_row(across, 1, 0)
    up0, down0 = add_halves(up0, down0, up1[4:], down1[4:])
    up0, down0, theirs = tie(up0, down0, theirs)
    up0, down0 = from_row(up0, 0, 3), from_row(down0, 0, 1)
    mine = add(mine, theirs).astype(BF16)
    mine, mate = tie(mine, core(mine))
    theirs, mate_theirs = pair(mine, "col", BF16, 4)[1], pair(mine, "col", BF16, 5)[1]
    here = add_across(own0, across)
    feature_grad, weight_grad, bias_grad = finish(here, up0, down0, meta, mine, theirs, mate, mate_theirs)
    return (activation, feature_grad, weight_grad, bias_grad.reshape(F))


def solution(mesh):
    in_specs = (
        P(("row", "col"), None),
        P(),
        P(),
        P(("row", "col"), None),
        P("row", "col", None, None),
        P("row", "col"),
        P("row", "col"),
        P("row", "col"),
    )
    out_specs = (P(("row", "col"), None), P(("row", "col"), None), P(), P())
    return jax.shard_map(
        per_device, mesh=mesh, in_specs=in_specs, out_specs=out_specs, check_vma=False
    )
```
